128 devices in a mesh: band: 16 (over z, x), pw: 8 (over y, core).
Axes of the slice: x: 4, y: 4, z: 4, core: 2. Of those that a mesh axis runs over, the one named last changes fastest.
Arguments:
- columns: bfloat16 [256, 8192, 256], P('band', 'pw'), may hold values from -2000 to 2000
- counts: int32 [8], replicated, may hold values from 1 to 1024, 6144 in all
Outputs:
- orthonormal: bfloat16 [256, 8192, 256], P('band', 'pw')
The draws below stay inside these ranges and needn't reach their ends.
Inputs may be any that keep to these rules, and one draw needn't show every extreme that they name: The counts add up to 6144, and the largest is exactly 1024.
All inputs are finite; a program needn't handle non-finite values.
Results may differ from the reference program's by a relative error of at most 0.0069.
Values may be sent and summed in bfloat16 or wider, within the bound.
No kernel may reach another device: no remote copies, remote signals or barrier semaphores. Data moves between devices by JAX's collectives and lax.ppermute only.
A program may use at most 128 MiB of HBM per device.

```python
import math
import jax
import jax.numpy as jnp
import numpy as np
from jax import lax

NB = 256
L = 256
CAP = 1024
ITERS = 8
NST = 6144
N_PW = 8


def draw_columns(key, part):
    key = jax.random.fold_in(key, 11)
    first, second, third, fourth = jax.random.split(key, 4)
    array_shape = (NB, CAP * N_PW, L)
    noise = jax.random.normal(first, array_shape, jnp.float32)
    strength = 0.35
    stick_scale = jnp.exp(jax.random.uniform(second, (1, CAP * N_PW, 1), jnp.float32, 0.0, 2.3))
    band_scale = jnp.exp(jax.random.uniform(third, (NB, 1, 1), jnp.float32, 0.0, 0.69))
    mixing = jnp.eye(NB, dtype=jnp.float32) + strength / jnp.sqrt(jnp.float32(NB)) * jax.random.normal(fourth, (NB, NB), jnp.float32)
    mixed = jnp.dot(mixing, noise.reshape(NB, -1), precision=lax.Precision.HIGHEST).reshape(array_shape)
    return (mixed * stick_scale * band_scale).astype(jnp.bfloat16)


def length_profile(amount, total, reach, slope):
    loads = [(1 << 20) // math.isqrt(standing ** slope) + 1 for standing in range(2, amount + 1)]
    spare, holding = total - reach - (amount - 1), [1] * (amount - 1)
    while spare > 0:
        free = [i for i in range(amount - 1) if holding[i] < reach]
        whole, left = sum([loads[i] for i in free]), spare
        for i in free:
            extra = min(reach - holding[i], max(1, left * loads[i] // whole), spare)
            holding[i] = holding[i] + extra
            spare = spare - extra
    return np.array([reach] + holding)


def ragged_sizes(key, count, total, most, skew):
    if count == 2:
        one = jax.random.randint(key, (), max(1, total - most), min(most, total - 1) + 1)
        return jnp.stack([one, total - one])
    sizes = jnp.asarray(length_profile(count, total, most, skew), jnp.int32)
    couples = (count - 1) // 2
    giver, sink = sizes[1:1 + 2 * couples:2], sizes[2:2 + 2 * couples:2]
    slack = jnp.minimum(giver - 1, most - sink)
    moved = jax.random.randint(jax.random.fold_in(key, 1), (couples,), 0, 1 << 20) % (slack + 1)
    sizes = sizes.at[1:1 + 2 * couples:2].set(giver - moved).at[2:2 + 2 * couples:2].set(sink + moved)
    return sizes[jax.random.permutation(jax.random.fold_in(key, 2), count)]


def setup_inputs(seed: int = 0) -> dict:
    key_list = jax.random.split(jax.random.key(seed), 3)
    return {
        "columns": draw_columns(jax.random.fold_in(key_list[2], 71), 0),
        "counts": ragged_sizes(key_list[1], N_PW, NST, CAP, 2).astype(jnp.int32),
    }


def hartley(stick_length):
    rows = jnp.arange(stick_length, dtype=jnp.int32)
    phase = (rows[:, None] * rows[None, :] % stick_length).astype(jnp.float32)
    angle = phase * (2.0 * jnp.pi / stick_length)
    return ((jnp.cos(angle) + jnp.sin(angle)) / jnp.sqrt(jnp.float32(stick_length))).astype(jnp.bfloat16)

def reference(columns, counts):
    band_count, total_slots, stick_length = columns.shape
    table = hartley(stick_length)
    slot_ids = jnp.arange(total_slots, dtype=jnp.int32)
    active_slots = slot_ids % CAP < counts[slot_ids // CAP]

    def transform(band):
        entry_value = jnp.dot(band, table, preferred_element_type=jnp.float32)
        return jnp.where(active_slots[:, None], entry_value, 0.0).astype(jnp.bfloat16)
    coeffs = lax.map(transform, columns)
    flat = coeffs.reshape(band_count, -1)
    partial_gram = lax.dot_general(flat, flat, (((1,), (1,)), ((), ())), preferred_element_type=jnp.float32)
    correlation = partial_gram / (jnp.sum(counts).astype(jnp.float32) * stick_length)
    scale = jnp.trace(correlation) / band_count
    ident = jnp.eye(band_count, dtype=jnp.float32)
    y_iter = correlation / scale
    z_iter = ident
    for step in range(ITERS):
        p_step = 1.5 * ident - 0.5 * jnp.dot(z_iter, y_iter, precision=lax.Precision.HIGHEST)
        y_iter = jnp.dot(y_iter, p_step, precision=lax.Precision.HIGHEST)
        z_iter = jnp.dot(p_step, z_iter, precision=lax.Precision.HIGHEST)
    rotation = (z_iter / jnp.sqrt(scale)).astype(jnp.bfloat16)
    rotated_bands = lax.dot_general(rotation, flat, (((0,), (0,)), ((), ())), preferred_element_type=jnp.float32)
    return rotated_bands.astype(jnp.bfloat16).reshape(band_count, total_slots, stick_length)
```

```python
import jax
import jax.numpy as jnp
import numpy as np
from jax import lax
from jax.experimental import pallas as pl
from jax.experimental.pallas import tpu as pltpu
from jax.sharding import PartitionSpec as P

ITERS = 8
GROUP = 16
HIGHEST = lax.Precision.HIGHEST
VMEM_LIMIT = 32 * 1024 * 1024


def hartley(stick_length):
    rows = np.arange(stick_length, dtype=np.int32)
    phase = (rows[:, None] * rows[None, :] % stick_length).astype(np.float32)
    angle = phase * np.float32(2.0 * np.pi / stick_length)
    table = (np.cos(angle) + np.sin(angle)) / np.sqrt(np.float32(stick_length))
    return jnp.asarray(table.astype(jnp.bfloat16))


def swap_matrix():
    size = GROUP * GROUP
    row = lax.broadcasted_iota(jnp.int32, (size, size), 0)
    col = lax.broadcasted_iota(jnp.int32, (size, size), 1)
    hit = (row % GROUP) * GROUP + row // GROUP == col
    return jnp.where(hit, 1.0, 0.0).astype(jnp.bfloat16)


def dot(left, right):
    return jnp.dot(left, right, preferred_element_type=jnp.float32)


def transform_kernel(counts_ref, table_ref, columns_ref, out_ref, swap_ref):
    step = pl.program_id(0)
    limit = counts_ref[lax.axis_index("pw")]
    slots = columns_ref.shape[1]
    length = columns_ref.shape[2]

    @pl.when(step == 0)
    def _():
        swap_ref[...] = swap_matrix()

    table = table_ref[...]
    swap = swap_ref[...]
    row_slot = lax.broadcasted_iota(jnp.int32, (GROUP * GROUP, length), 0) // GROUP
    for part in range(slots // GROUP):
        base = step * slots + part * GROUP
        block = columns_ref[:, part * GROUP : (part + 1) * GROUP, :].reshape(-1, length)
        turned = dot(swap, block).astype(jnp.bfloat16)
        value = dot(turned, table)
        value = jnp.where(row_slot < limit - base, value, 0.0).astype(jnp.bfloat16)
        out_ref[0, part * GROUP : (part + 1) * GROUP, :, :] = value.reshape(GROUP, GROUP, length)


def transform(columns, counts, members):
    bands, slots, length = columns.shape
    each = slots // members
    return pl.pallas_call(
        transform_kernel,
        grid=(members,),
        in_specs=[
            pl.BlockSpec(memory_space=pltpu.SMEM),
            pl.BlockSpec((length, length), lambda i: (0, 0)),
            pl.BlockSpec((bands, each, length), lambda i: (0, i, 0)),
        ],
        out_specs=pl.BlockSpec((1, each, bands, length), lambda i: (i, 0, 0, 0)),
        out_shape=jax.ShapeDtypeStruct((members, each, bands, length), jnp.bfloat16),
        scratch_shapes=[pltpu.VMEM((GROUP * GROUP, GROUP * GROUP), jnp.bfloat16)],
        compiler_params=pltpu.CompilerParams(vmem_limit_bytes=VMEM_LIMIT),
        name="transform",
    )(counts, hartley(length), columns)


def gram_kernel(sticks_ref, out_ref):
    @pl.when(pl.program_id(0) == 0)
    def _():
        out_ref[...] = jnp.zeros_like(out_ref)

    members, slots, bands, length = sticks_ref.shape
    rows = [sticks_ref[:, s].reshape(members * bands, length) for s in range(slots)]
    wide = jnp.concatenate(rows, axis=1)
    out_ref[...] += lax.dot_general(
        wide, wide, (((1,), (1,)), ((), ())), preferred_element_type=jnp.float32
    )


def gram(sticks, each):
    members, slots, bands, length = sticks.shape
    total = members * bands
    return pl.pallas_call(
        gram_kernel,
        grid=(slots // each,),
        in_specs=[pl.BlockSpec((members, each, bands, length), lambda i: (0, i, 0, 0))],
        out_specs=pl.BlockSpec((total, total), lambda i: (0, 0)),
        out_shape=jax.ShapeDtypeStruct((total, total), jnp.float32),
        compiler_params=pltpu.CompilerParams(vmem_limit_bytes=VMEM_LIMIT),
        name="gram",
    )(sticks)


def rotate_kernel(rotation_ref, sticks_ref, out_ref):
    members, slots, bands, length = sticks_ref.shape
    turn = rotation_ref[...]
    for s in range(slots):
        rows = sticks_ref[:, s].reshape(members * bands, length)
        out_ref[:, s] = dot(turn, rows).astype(jnp.bfloat16).reshape(members, bands, length)


def rotate(rotation_t, sticks, each):
    members, slots, bands, length = sticks.shape
    total = members * bands
    block = pl.BlockSpec((members, each, bands, length), lambda i: (0, i, 0, 0))
    return pl.pallas_call(
        rotate_kernel,
        grid=(slots // each,),
        in_specs=[pl.BlockSpec((total, total), lambda i: (0, 0)), block],
        out_specs=block,
        out_shape=jax.ShapeDtypeStruct(sticks.shape, jnp.bfloat16),
        compiler_params=pltpu.CompilerParams(vmem_limit_bytes=VMEM_LIMIT),
        name="rotate",
    )(rotation_t, sticks)


def place_kernel(in_ref, out_ref, swap_ref):
    @pl.when(pl.program_id(0) == 0)
    def _():
        swap_ref[...] = swap_matrix()

    _, slots, bands, length = in_ref.shape
    swap = swap_ref[...]
    for part in range(slots // GROUP):
        block = in_ref[0, part * GROUP : (part + 1) * GROUP].reshape(-1, length)
        turned = dot(swap, block).astype(jnp.bfloat16)
        out_ref[:, part * GROUP : (part + 1) * GROUP, :] = turned.reshape(bands, GROUP, length)


def place(rotated):
    members, slots, bands, length = rotated.shape
    return pl.pallas_call(
        place_kernel,
        grid=(members,),
        in_specs=[pl.BlockSpec((1, slots, bands, length), lambda i: (i, 0, 0, 0))],
        out_specs=pl.BlockSpec((bands, slots, length), lambda i: (0, i, 0)),
        out_shape=jax.ShapeDtypeStruct((bands, members * slots, length), jnp.bfloat16),
        scratch_shapes=[pltpu.VMEM((GROUP * GROUP, GROUP * GROUP), jnp.bfloat16)],
        compiler_params=pltpu.CompilerParams(vmem_limit_bytes=VMEM_LIMIT),
        name="place",
    )(rotated)


def matmul(left, right):
    return jnp.dot(left, right, precision=HIGHEST)


def whole_sum(part, axes, devices):
    rows, cols = part.shape
    shares = part.reshape(devices, rows // devices, cols)
    share = lax.all_to_all(shares, axes, 0, 0, tiled=True).sum(0)
    spread = jnp.broadcast_to(share[None], shares.shape)
    return lax.all_to_all(spread, axes, 0, 0, tiled=True).reshape(rows, cols)


def make_local(members, devices):
    def local(columns, counts):
        stick_length = columns.shape[2]
        send = transform(columns, counts, members)
        sticks = lax.all_to_all(send, "band", 0, 0, tiled=True)
        total = whole_sum(gram(sticks, 8), ("band", "pw"), devices)
        norming = jnp.sum(counts).astype(jnp.float32) * stick_length
        correlation = total / norming
        band_count = correlation.shape[0]
        scale = jnp.trace(correlation) / band_count
        ident = jnp.eye(band_count, dtype=jnp.float32)
        y_iter = correlation / scale
        z_iter = ident
        for step in range(ITERS):
            p_step = 1.5 * ident - 0.5 * matmul(z_iter, y_iter)
            y_iter = matmul(y_iter, p_step)
            z_iter = matmul(p_step, z_iter)
        rotation = (z_iter / jnp.sqrt(scale)).astype(jnp.bfloat16)
        rotated = rotate(rotation.T, sticks, 8)
        return place(lax.all_to_all(rotated, "band", 0, 0, tiled=True))

    return local


def solution(mesh):
    members = mesh.shape["band"]
    return jax.shard_map(
        make_local(members, mesh.size),
        mesh=mesh,
        in_specs=(P("band", "pw", None), P()),
        out_specs=P("band", "pw", None),
        check_vma=False,
    )
```

```python
import functools

import jax
import jax.numpy as jnp
import numpy as np
from jax import lax
from jax.experimental import pallas as pl
from jax.experimental.pallas import tpu as pltpu
from jax.sharding import PartitionSpec as P

ITERS = 8
GROUP = 16
MIB = 1024 * 1024


def hartley(stick_length):
    rows = np.arange(stick_length, dtype=np.int32)
    phase = (rows[:, None] * rows[None, :] % stick_length).astype(np.float32)
    angle = phase * np.float32(2.0 * np.pi / stick_length)
    table = (np.cos(angle) + np.sin(angle)) / np.sqrt(np.float32(stick_length))
    return jnp.asarray(table.astype(jnp.bfloat16))


def dot(left, right):
    return jnp.dot(left, right, preferred_element_type=jnp.float32)


def params(mib):
    return pltpu.CompilerParams(vmem_limit_bytes=mib * MIB)


def transform_kernel(counts_ref, table_ref, columns_ref, out_ref, buf, table, sems, table_sem):
    members, each, bands, length = out_ref.shape

    def fetch(i):
        rows = pl.ds(pl.multiple_of(i * each, each), each)
        return pltpu.make_async_copy(columns_ref.at[:, rows, :], buf.at[i], sems.at[i])

    table_copy = pltpu.make_async_copy(table_ref, table, table_sem)
    table_copy.start()
    for i in range(members):
        fetch(i).start()
    limit = counts_ref[lax.axis_index("pw")]
    row_slot = lax.broadcasted_iota(jnp.int32, (each * bands, length), 0) // bands
    table_copy.wait()

    def step(i, carry):
        fetch(i).wait()
        turned = [
            jnp.swapaxes(buf[i, :, s : s + GROUP, :], 0, 1).reshape(GROUP * bands, length)
            for s in range(0, each, GROUP)
        ]
        value = dot(jnp.concatenate(turned, axis=0), table[...])
        value = jnp.where(row_slot < limit - i * each, value, 0.0).astype(jnp.bfloat16)
        out_ref[i] = value.reshape(each, bands, length)
        return carry

    lax.fori_loop(0, members, step, 0)


def transform(columns, counts, members):
    bands, slots, length = columns.shape
    each = slots // members
    return pl.pallas_call(
        transform_kernel,
        in_specs=[
            pl.BlockSpec(memory_space=pltpu.SMEM),
            pl.BlockSpec(memory_space=pltpu.HBM),
            pl.BlockSpec(memory_space=pltpu.HBM),
        ],
        out_specs=pl.BlockSpec(memory_space=pltpu.VMEM),
        out_shape=jax.ShapeDtypeStruct((members, each, bands, length), jnp.bfloat16),
        scratch_shapes=[
            pltpu.VMEM((members, bands, each, length), jnp.bfloat16),
            pltpu.VMEM((length, length), jnp.bfloat16),
            pltpu.SemaphoreType.DMA((members,)),
            pltpu.SemaphoreType.DMA,
        ],
        compiler_params=params(44),
        name="transform",
    )(counts, hartley(length), columns)


def fetch_slots(sticks_ref, buf, sems, i, each):
    rows = pl.ds(i * each, each)
    return pltpu.make_async_copy(sticks_ref.at[:, rows], buf.at[:, rows], sems.at[i])


def gram_kernel(each, sticks_ref, out_ref, buf, sems):
    members, slots, bands, length = sticks_ref.shape
    total = members * bands
    steps = slots // each
    for i in range(steps):
        fetch_slots(sticks_ref, buf, sems, i, each).start()
    acc = jnp.zeros((total, total), jnp.float32)
    for i in range(steps):
        fetch_slots(sticks_ref, buf, sems, i, each).wait()
        rows = [buf[:, i * each + s].reshape(total, length) for s in range(each)]
        wide = jnp.concatenate(rows, axis=1)
        acc += lax.dot_general(
            wide, wide, (((1,), (1,)), ((), ())), preferred_element_type=jnp.float32
        )
    piece = 0
    for r in range(0, total, 8):
        for c in range(0, total, 128):
            for half in range(2):
                out_ref[piece] = acc[r + 4 * half : r + 4 * half + 4, c : c + 128]
                piece += 1


def gram(sticks, each):
    members, slots, bands, length = sticks.shape
    total = members * bands
    return pl.pallas_call(
        functools.partial(gram_kernel, each),
        in_specs=[pl.BlockSpec(memory_space=pltpu.HBM)],
        out_specs=pl.BlockSpec(memory_space=pltpu.VMEM),
        out_shape=jax.ShapeDtypeStruct((total * total // 512, 4, 128), jnp.float32),
        scratch_shapes=[
            pltpu.VMEM(sticks.shape, jnp.bfloat16),
            pltpu.SemaphoreType.DMA((slots // each,)),
        ],
        compiler_params=params(52),
        name="gram",
    )(sticks)


def split(value):
    high = value.astype(jnp.bfloat16)
    return high, (value - high.astype(jnp.float32)).astype(jnp.bfloat16)


def product(left, right):
    left_high, left_low = left
    right_high, right_low = right
    return dot(left_high, right_high) + (dot(left_high, right_low) + dot(left_low, right_high))


def rotate_kernel(each, counts_ref, sums_ref, sticks_ref, out_ref, buf, sems, turn_ref):
    members, slots, bands, length = sticks_ref.shape
    size = members * bands
    steps = slots // each
    for i in range(steps):
        fetch_slots(sticks_ref, buf, sems, i, each).start()

    live = counts_ref[0]
    for i in range(1, counts_ref.shape[0]):
        live += counts_ref[i]
    tiles = size // 128
    pieces = [sums_ref[i] for i in range(sums_ref.shape[0])]
    whole = [jnp.concatenate(pieces[i : i + 2], axis=0) for i in range(0, len(pieces), 2)]
    lines = [jnp.concatenate(whole[i : i + tiles], axis=1) for i in range(0, len(whole), tiles)]
    correlation = jnp.concatenate(lines, axis=0) / (live.astype(jnp.float32) * length)
    row = lax.broadcasted_iota(jnp.int32, (size, size), 0)
    col = lax.broadcasted_iota(jnp.int32, (size, size), 1)
    ident = jnp.where(row == col, 1.0, 0.0)
    scale = jnp.sum(correlation * ident, keepdims=True) / size
    y_iter = correlation / scale

    z_iter = 1.5 * ident - 0.5 * y_iter
    z_split = split(z_iter)
    y_split = split(product(split(y_iter), z_split))
    for step in range(1, ITERS):
        p_split = split(1.5 * ident - 0.5 * product(z_split, y_split))
        if step < ITERS - 1:
            y_split = split(product(y_split, p_split))
        z_iter = product(p_split, z_split)
        z_split = split(z_iter)
    turn_ref[...] = (z_iter / jnp.sqrt(scale)).T.astype(jnp.bfloat16)

    turn = turn_ref[...]
    for i in range(steps):
        fetch_slots(sticks_ref, buf, sems, i, each).wait()
    for i in range(steps):
        for s in range(i * each, (i + 1) * each):
            value = dot(turn, buf[:, s].reshape(size, length)).astype(jnp.bfloat16)
            out_ref[:, s] = value.reshape(members, bands, length)


def rotate(counts, sums, sticks, each):
    members, slots, bands, length = sticks.shape
    size = members * bands
    return pl.pallas_call(
        functools.partial(rotate_kernel, each),
        in_specs=[
            pl.BlockSpec(memory_space=pltpu.SMEM),
            pl.BlockSpec(memory_space=pltpu.VMEM),
            pl.BlockSpec(memory_space=pltpu.HBM),
        ],
        out_specs=pl.BlockSpec(memory_space=pltpu.VMEM),
        out_shape=jax.ShapeDtypeStruct(sticks.shape, jnp.bfloat16),
        scratch_shapes=[
            pltpu.VMEM(sticks.shape, jnp.bfloat16),
            pltpu.SemaphoreType.DMA((slots // each,)),
            pltpu.VMEM((size, size), jnp.bfloat16),
        ],
        compiler_params=params(44),
        name="rotate",
    )(counts, sums, sticks)


def place_kernel(in_ref, out_ref, buf, sems):
    members, each, bands, length = in_ref.shape

    def store(i):
        rows = pl.ds(pl.multiple_of(i * each, each), each)
        return pltpu.make_async_copy(buf.at[i], out_ref.at[:, rows, :], sems.at[i])

    def step(i, carry):
        for s in range(0, each, GROUP):
            buf[i, :, s : s + GROUP, :] = jnp.swapaxes(in_ref[i, s : s + GROUP], 0, 1)
        store(i).start()
        return carry

    def finish(i, carry):
        store(i).wait()
        return carry

    lax.fori_loop(0, members, step, 0)
    lax.fori_loop(0, members, finish, 0)


def place(rotated):
    members, each, bands, length = rotated.shape
    return pl.pallas_call(
        place_kernel,
        in_specs=[pl.BlockSpec(memory_space=pltpu.VMEM)],
        out_specs=pl.BlockSpec(memory_space=pltpu.HBM),
        out_shape=jax.ShapeDtypeStruct((bands, members * each, length), jnp.bfloat16),
        scratch_shapes=[
            pltpu.VMEM((members, bands, each, length), jnp.bfloat16),
            pltpu.SemaphoreType.DMA((members,)),
        ],
        compiler_params=params(32),
        name="place",
    )(rotated)


def whole_sum(shares, axes):
    share = lax.all_to_all(shares, axes, 0, 0, tiled=True).sum(0)
    spread = jnp.broadcast_to(share[None], shares.shape)
    return lax.all_to_all(spread, axes, 0, 0, tiled=True)


def make_local(members):
    def local(columns, counts):
        send = transform(columns, counts, members)
        sticks = lax.all_to_all(send, "band", 0, 0, tiled=True)
        sums = whole_sum(gram(sticks, 8), ("band", "pw"))
        rotated = rotate(counts, sums, sticks, 16)
        return place(lax.all_to_all(rotated, "band", 0, 0, tiled=True))

    return local


def solution(mesh):
    return jax.shard_map(
        make_local(mesh.shape["band"]),
        mesh=mesh,
        in_specs=(P("band", "pw", None), P()),
        out_specs=P("band", "pw", None),
        check_vma=False,
    )
```

```python
import functools

import jax
import jax.numpy as jnp
import numpy as np
from jax import lax
from jax.experimental import pallas as pl
from jax.experimental.pallas import tpu as pltpu
from jax.sharding import PartitionSpec as P

ITERS = 8
GROUP = 16
MIB = 1024 * 1024


def hartley(stick_length):
    rows = np.arange(stick_length, dtype=np.int32)
    phase = (rows[:, None] * rows[None, :] % stick_length).astype(np.float32)
    angle = phase * np.float32(2.0 * np.pi / stick_length)
    table = (np.cos(angle) + np.sin(angle)) / np.sqrt(np.float32(stick_length))
    return jnp.asarray(table.astype(jnp.bfloat16))


def dot(left, right):
    return jnp.dot(left, right, preferred_element_type=jnp.float32)


def params(mib):
    return pltpu.CompilerParams(vmem_limit_bytes=mib * MIB)


def transform_kernel(counts_ref, table_ref, columns_ref, out_ref, buf, table, sems, table_sem):
    members, each, bands, length = out_ref.shape
    steps = buf.shape[0]
    span = buf.shape[2]
    per_member = each // GROUP

    def fetch(i):
        rows = pl.ds(pl.multiple_of(i * span, span), span)
        return pltpu.make_async_copy(columns_ref.at[:, rows, :], buf.at[i], sems.at[i])

    table_copy = pltpu.make_async_copy(table_ref, table, table_sem)
    table_copy.start()
    for i in range(steps):
        fetch(i).start()
    limit = counts_ref[lax.axis_index("pw")]
    row_slot = lax.broadcasted_iota(jnp.int32, (GROUP * bands, length), 0) // bands
    table_copy.wait()

    def step(i, carry):
        fetch(i).wait()
        for part in range(span // GROUP):
            rows = slice(part * GROUP, (part + 1) * GROUP)
            turned = jnp.swapaxes(buf[i, :, rows, :], 0, 1).reshape(GROUP * bands, length)
            value = dot(turned, table[...])
            value = jnp.where(row_slot < limit - (i * span + part * GROUP), value, 0.0)
            value = value.astype(jnp.bfloat16).reshape(GROUP, bands, length)
            member = i * (span // each) + part // per_member
            first = part % per_member * GROUP
            out_ref[member, first : first + GROUP] = value
        return carry

    lax.fori_loop(0, steps, step, 0)


def transform(columns, counts, members):
    bands, slots, length = columns.shape
    each = slots // members
    span = 2 * each
    steps = slots // span
    return pl.pallas_call(
        transform_kernel,
        in_specs=[
            pl.BlockSpec(memory_space=pltpu.SMEM),
            pl.BlockSpec(memory_space=pltpu.HBM),
            pl.BlockSpec(memory_space=pltpu.HBM),
        ],
        out_specs=pl.BlockSpec(memory_space=pltpu.VMEM),
        out_shape=jax.ShapeDtypeStruct((members, each, bands, length), jnp.bfloat16),
        scratch_shapes=[
            pltpu.VMEM((steps, bands, span, length), jnp.bfloat16),
            pltpu.VMEM((length, length), jnp.bfloat16),
            pltpu.SemaphoreType.DMA((steps,)),
            pltpu.SemaphoreType.DMA,
        ],
        compiler_params=params(44),
        name="transform",
    )(counts, hartley(length), columns)


def gram_kernel(each, sticks_ref, out_ref):
    members, slots, bands, length = sticks_ref.shape
    total = members * bands
    acc = jnp.zeros((total, total), jnp.float32)
    for i in range(0, slots, each):
        rows = [sticks_ref[:, i + s].reshape(total, length) for s in range(each)]
        wide = jnp.concatenate(rows, axis=1)
        acc += lax.dot_general(
            wide, wide, (((1,), (1,)), ((), ())), preferred_element_type=jnp.float32
        )
    piece = 0
    for r in range(0, total, 8):
        for c in range(0, total, 128):
            for half in range(2):
                out_ref[piece] = acc[r + 4 * half : r + 4 * half + 4, c : c + 128]
                piece += 1


def gram(sticks, each):
    members, slots, bands, length = sticks.shape
    total = members * bands
    return pl.pallas_call(
        functools.partial(gram_kernel, each),
        in_specs=[pl.BlockSpec(memory_space=pltpu.VMEM)],
        out_specs=pl.BlockSpec(memory_space=pltpu.VMEM),
        out_shape=jax.ShapeDtypeStruct((total * total // 512, 4, 128), jnp.float32),
        compiler_params=params(20),
        name="gram",
    )(sticks)


def spread_kernel(shares_ref, out_ref):
    share = jnp.sum(shares_ref[...], axis=0, keepdims=True)
    out_ref[...] = jnp.broadcast_to(share, out_ref.shape)


def spread(shares):
    return pl.pallas_call(
        spread_kernel,
        in_specs=[pl.BlockSpec(memory_space=pltpu.VMEM)],
        out_specs=pl.BlockSpec(memory_space=pltpu.VMEM),
        out_shape=jax.ShapeDtypeStruct(shares.shape, shares.dtype),
        compiler_params=params(8),
        name="spread",
    )(shares)


def split(value):
    high = value.astype(jnp.bfloat16)
    return high, (value - high.astype(jnp.float32)).astype(jnp.bfloat16)


def product(left, right):
    left_high, left_low = left
    right_high, right_low = right
    return dot(left_high, right_high) + (dot(left_high, right_low) + dot(left_low, right_high))


def rotate_kernel(counts_ref, sums_ref, sticks_ref, out_ref, turn_ref):
    members, slots, bands, length = sticks_ref.shape
    size = members * bands
    live = counts_ref[0]
    for i in range(1, counts_ref.shape[0]):
        live += counts_ref[i]
    tiles = size // 128
    pieces = [sums_ref[i] for i in range(sums_ref.shape[0])]
    whole = [jnp.concatenate(pieces[i : i + 2], axis=0) for i in range(0, len(pieces), 2)]
    lines = [jnp.concatenate(whole[i : i + tiles], axis=1) for i in range(0, len(whole), tiles)]
    correlation = jnp.concatenate(lines, axis=0) / (live.astype(jnp.float32) * length)
    row = lax.broadcasted_iota(jnp.int32, (size, size), 0)
    col = lax.broadcasted_iota(jnp.int32, (size, size), 1)
    ident = jnp.where(row == col, 1.0, 0.0)
    scale = jnp.sum(correlation * ident, keepdims=True) / size
    y_iter = correlation / scale

    z_iter = 1.5 * ident - 0.5 * y_iter
    z_split = split(z_iter)
    y_split = split(product(split(y_iter), z_split))
    for step in range(1, ITERS):
        p_split = split(1.5 * ident - 0.5 * product(z_split, y_split))
        if step < ITERS - 1:
            y_split = split(product(y_split, p_split))
        z_iter = product(p_split, z_split)
        z_split = split(z_iter)
    turn_ref[...] = (z_iter / jnp.sqrt(scale)).T.astype(jnp.bfloat16)

    turn = turn_ref[...]
    for s in range(slots):
        value = dot(turn, sticks_ref[:, s].reshape(size, length)).astype(jnp.bfloat16)
        out_ref[:, s] = value.reshape(members, bands, length)


def rotate(counts, sums, sticks):
    members, slots, bands, length = sticks.shape
    size = members * bands
    return pl.pallas_call(
        rotate_kernel,
        in_specs=[
            pl.BlockSpec(memory_space=pltpu.SMEM),
            pl.BlockSpec(memory_space=pltpu.VMEM),
            pl.BlockSpec(memory_space=pltpu.VMEM),
        ],
        out_specs=pl.BlockSpec(memory_space=pltpu.VMEM),
        out_shape=jax.ShapeDtypeStruct(sticks.shape, jnp.bfloat16),
        scratch_shapes=[pltpu.VMEM((size, size), jnp.bfloat16)],
        compiler_params=params(24),
        name="rotate",
    )(counts, sums, sticks)


def place_kernel(in_ref, out_ref, buf, sems):
    members, each, bands, length = in_ref.shape

    def store(i):
        rows = pl.ds(pl.multiple_of(i * each, each), each)
        return pltpu.make_async_copy(buf.at[i], out_ref.at[:, rows, :], sems.at[i])

    def step(i, carry):
        for s in range(0, each, GROUP):
            buf[i, :, s : s + GROUP, :] = jnp.swapaxes(in_ref[i, s : s + GROUP], 0, 1)
        store(i).start()
        return carry

    def finish(i, carry):
        store(i).wait()
        return carry

    lax.fori_loop(0, members, step, 0)
    lax.fori_loop(0, members, finish, 0)


def place(rotated):
    members, each, bands, length = rotated.shape
    return pl.pallas_call(
        place_kernel,
        in_specs=[pl.BlockSpec(memory_space=pltpu.VMEM)],
        out_specs=pl.BlockSpec(memory_space=pltpu.HBM),
        out_shape=jax.ShapeDtypeStruct((bands, members * each, length), jnp.bfloat16),
        scratch_shapes=[
            pltpu.VMEM((members, bands, each, length), jnp.bfloat16),
            pltpu.SemaphoreType.DMA((members,)),
        ],
        compiler_params=params(32),
        name="place",
    )(rotated)


def make_local(members):
    def local(columns, counts):
        def exchange(value, axes):
            return lax.all_to_all(value, axes, 0, 0, tiled=True)

        sticks = exchange(transform(columns, counts, members), "band")
        shares = exchange(gram(sticks, 16), ("band", "pw"))
        sums = exchange(spread(shares), ("band", "pw"))
        return place(exchange(rotate(counts, sums, sticks), "band"))

    return local


def solution(mesh):
    return jax.shard_map(
        make_local(mesh.shape["band"]),
        mesh=mesh,
        in_specs=(P("band", "pw", None), P()),
        out_specs=P("band", "pw", None),
        check_vma=False,
    )
```

```python
import functools

import jax
import jax.numpy as jnp
import numpy as np
from jax import lax
from jax.experimental import pallas as pl
from jax.experimental.pallas import tpu as pltpu
from jax.sharding import PartitionSpec as P

ITERS = 8
GROUP = 16
MIB = 1024 * 1024


def hartley(stick_length):
    rows = np.arange(stick_length, dtype=np.int32)
    phase = (rows[:, None] * rows[None, :] % stick_length).astype(np.float32)
    angle = phase * np.float32(2.0 * np.pi / stick_length)
    table = (np.cos(angle) + np.sin(angle)) / np.sqrt(np.float32(stick_length))
    return jnp.asarray(table.astype(jnp.bfloat16))


def dot(left, right):
    return jnp.dot(left, right, preferred_element_type=jnp.float32)


def params(mib):
    return pltpu.CompilerParams(vmem_limit_bytes=mib * MIB)


def in_hbm(value):
    return pltpu.with_memory_space_constraint(value, pltpu.HBM)


def transform_kernel(counts_ref, table_ref, columns_ref, out_ref, buf, table, limits, *sems):
    members, each, bands, length = out_ref.shape
    steps = buf.shape[0]
    span = buf.shape[2]
    per_member = each // GROUP
    read_sems, table_sem, counts_sem = sems

    def fetch(i):
        rows = pl.ds(pl.multiple_of(i * span, span), span)
        return pltpu.make_async_copy(columns_ref.at[:, rows, :], buf.at[i], read_sems.at[i])

    counts_copy = pltpu.make_async_copy(counts_ref, limits, counts_sem)
    table_copy = pltpu.make_async_copy(table_ref, table, table_sem)
    counts_copy.start()
    table_copy.start()
    for i in range(steps):
        fetch(i).start()
    row_slot = lax.broadcasted_iota(jnp.int32, (GROUP * bands, length), 0) // bands
    counts_copy.wait()
    table_copy.wait()
    limit = limits[lax.axis_index("pw")]

    def groups(i):
        for part in range(span // GROUP):
            first = part % per_member * GROUP
            member = i * (span // each) + part // per_member
            yield part * GROUP, (member, slice(first, first + GROUP))

    def step(i, carry):
        fetch(i).wait()
        left = limit - i * span

        def value(start):
            rows = buf[i, :, start : start + GROUP, :]
            turned = jnp.swapaxes(rows, 0, 1).reshape(GROUP * bands, length)
            return dot(turned, table[...])

        def put(at, rows):
            out_ref[at] = rows.astype(jnp.bfloat16).reshape(GROUP, bands, length)

        @pl.when(left >= span)
        def _():
            for start, at in groups(i):
                put(at, value(start))

        @pl.when(left < span)
        def _():
            for start, at in groups(i):
                put(at, jnp.where(row_slot < left - start, value(start), 0.0))

        return carry

    lax.fori_loop(0, steps, step, 0)


def transform(columns, counts, members):
    bands, slots, length = columns.shape
    each = slots // members
    span = 2 * each
    steps = slots // span
    return pl.pallas_call(
        transform_kernel,
        in_specs=[pl.BlockSpec(memory_space=pltpu.HBM)] * 3,
        out_specs=pl.BlockSpec(memory_space=pltpu.VMEM),
        out_shape=jax.ShapeDtypeStruct((members, each, bands, length), jnp.bfloat16),
        scratch_shapes=[
            pltpu.VMEM((steps, bands, span, length), jnp.bfloat16),
            pltpu.VMEM((length, length), jnp.bfloat16),
            pltpu.SMEM(counts.shape, jnp.int32),
            pltpu.SemaphoreType.DMA((steps,)),
            pltpu.SemaphoreType.DMA,
            pltpu.SemaphoreType.DMA,
        ],
        compiler_params=params(44),
        name="transform",
    )(in_hbm(counts), in_hbm(hartley(length)), in_hbm(columns))


def gram_kernel(each, sticks_ref, out_ref):
    members, slots, bands, length = sticks_ref.shape
    total = members * bands
    acc = jnp.zeros((total, total), jnp.float32)
    for i in range(0, slots, each):
        rows = [sticks_ref[:, i + s].reshape(total, length) for s in range(each)]
        wide = jnp.concatenate(rows, axis=1)
        acc += lax.dot_general(
            wide, wide, (((1,), (1,)), ((), ())), preferred_element_type=jnp.float32
        )
    piece = 0
    for r in range(0, total, 8):
        for c in range(0, total, 128):
            for half in range(2):
                out_ref[piece] = acc[r + 4 * half : r + 4 * half + 4, c : c + 128]
                piece += 1


def gram(sticks, each):
    members, slots, bands, length = sticks.shape
    total = members * bands
    return pl.pallas_call(
        functools.partial(gram_kernel, each),
        in_specs=[pl.BlockSpec(memory_space=pltpu.VMEM)],
        out_specs=pl.BlockSpec(memory_space=pltpu.VMEM),
        out_shape=jax.ShapeDtypeStruct((total * total // 512, 4, 128), jnp.float32),
        compiler_params=params(20),
        name="gram",
    )(sticks)


def spread_kernel(shares_ref, out_ref):
    share = jnp.sum(shares_ref[...], axis=0, keepdims=True)
    out_ref[...] = jnp.broadcast_to(share, out_ref.shape)


def spread(shares):
    return pl.pallas_call(
        spread_kernel,
        in_specs=[pl.BlockSpec(memory_space=pltpu.VMEM)],
        out_specs=pl.BlockSpec(memory_space=pltpu.VMEM),
        out_shape=jax.ShapeDtypeStruct(shares.shape, shares.dtype),
        compiler_params=params(8),
        name="spread",
    )(shares)


def split(value):
    high = value.astype(jnp.bfloat16)
    return high, (value - high.astype(jnp.float32)).astype(jnp.bfloat16)


def product(left, right):
    left_high, left_low = left
    right_high, right_low = right
    return dot(left_high, right_high) + (dot(left_high, right_low) + dot(left_low, right_high))


def rotate_kernel(counts_ref, sums_ref, sticks_ref, out_ref, turn_ref):
    members, slots, bands, length = sticks_ref.shape
    size = members * bands
    live = counts_ref[0]
    for i in range(1, counts_ref.shape[0]):
        live += counts_ref[i]
    tiles = size // 128
    pieces = [sums_ref[i] for i in range(sums_ref.shape[0])]
    whole = [jnp.concatenate(pieces[i : i + 2], axis=0) for i in range(0, len(pieces), 2)]
    lines = [jnp.concatenate(whole[i : i + tiles], axis=1) for i in range(0, len(whole), tiles)]
    correlation = jnp.concatenate(lines, axis=0) / (live.astype(jnp.float32) * length)
    row = lax.broadcasted_iota(jnp.int32, (size, size), 0)
    col = lax.broadcasted_iota(jnp.int32, (size, size), 1)
    ident = jnp.where(row == col, 1.0, 0.0)
    scale = jnp.sum(correlation * ident, keepdims=True) / size
    y_iter = correlation / scale

    z_iter = 1.5 * ident - 0.5 * y_iter
    z_split = split(z_iter)
    y_split = split(product(split(y_iter), z_split))
    for step in range(1, ITERS):
        p_split = split(1.5 * ident - 0.5 * product(z_split, y_split))
        if step < ITERS - 1:
            y_split = split(product(y_split, p_split))
        z_iter = product(p_split, z_split)
        z_split = split(z_iter)
    turn_ref[...] = (z_iter / jnp.sqrt(scale)).T.astype(jnp.bfloat16)

    turn = turn_ref[...]
    for s in range(slots):
        value = dot(turn, sticks_ref[:, s].reshape(size, length)).astype(jnp.bfloat16)
        out_ref[:, s] = value.reshape(members, bands, length)


def rotate(counts, sums, sticks):
    members, slots, bands, length = sticks.shape
    size = members * bands
    return pl.pallas_call(
        rotate_kernel,
        in_specs=[
            pl.BlockSpec(memory_space=pltpu.SMEM),
            pl.BlockSpec(memory_space=pltpu.VMEM),
            pl.BlockSpec(memory_space=pltpu.VMEM),
        ],
        out_specs=pl.BlockSpec(memory_space=pltpu.VMEM),
        out_shape=jax.ShapeDtypeStruct(sticks.shape, jnp.bfloat16),
        scratch_shapes=[pltpu.VMEM((size, size), jnp.bfloat16)],
        compiler_params=params(24),
        name="rotate",
    )(counts, sums, sticks)


def place_kernel(in_ref, out_ref, buf, sems):
    members, each, bands, length = in_ref.shape

    def store(i):
        rows = pl.ds(pl.multiple_of(i * each, each), each)
        return pltpu.make_async_copy(buf.at[i], out_ref.at[:, rows, :], sems.at[i])

    def step(i, carry):
        for s in range(0, each, GROUP):
            buf[i, :, s : s + GROUP, :] = jnp.swapaxes(in_ref[i, s : s + GROUP], 0, 1)
        store(i).start()
        return carry

    def finish(i, carry):
        store(i).wait()
        return carry

    lax.fori_loop(0, members, step, 0)
    lax.fori_loop(0, members, finish, 0)


def place(rotated):
    members, each, bands, length = rotated.shape
    return pl.pallas_call(
        place_kernel,
        in_specs=[pl.BlockSpec(memory_space=pltpu.VMEM)],
        out_specs=pl.BlockSpec(memory_space=pltpu.HBM),
        out_shape=jax.ShapeDtypeStruct((bands, members * each, length), jnp.bfloat16),
        scratch_shapes=[
            pltpu.VMEM((members, bands, each, length), jnp.bfloat16),
            pltpu.SemaphoreType.DMA((members,)),
        ],
        compiler_params=params(32),
        name="place",
    )(rotated)


def make_local(members):
    def local(columns, counts):
        def exchange(value, axes):
            return lax.all_to_all(value, axes, 0, 0, tiled=True)

        sticks = exchange(transform(columns, counts, members), "band")
        shares = exchange(gram(sticks, 16), ("band", "pw"))
        sums = exchange(spread(shares), ("band", "pw"))
        return place(exchange(rotate(counts, sums, sticks), "band"))

    return local


def solution(mesh):
    return jax.shard_map(
        make_local(mesh.shape["band"]),
        mesh=mesh,
        in_specs=(P("band", "pw", None), P()),
        out_specs=P("band", "pw", None),
        check_vma=False,
    )
```

```python
import functools

import jax
import jax.numpy as jnp
import numpy as np
from jax import lax
from jax.experimental import pallas as pl
from jax.experimental.pallas import tpu as pltpu
from jax.sharding import PartitionSpec as P

ITERS = 8
GROUP = 16
MIB = 1024 * 1024


def hartley(stick_length):
    rows = np.arange(stick_length, dtype=np.int32)
    phase = (rows[:, None] * rows[None, :] % stick_length).astype(np.float32)
    angle = phase * np.float32(2.0 * np.pi / stick_length)
    table = (np.cos(angle) + np.sin(angle)) / np.sqrt(np.float32(stick_length))
    return jnp.asarray(table.astype(jnp.bfloat16))


def dot(left, right):
    return jnp.dot(left, right, preferred_element_type=jnp.float32)


def params(mib):
    return pltpu.CompilerParams(vmem_limit_bytes=mib * MIB)


def in_hbm(value):
    return pltpu.with_memory_space_constraint(value, pltpu.HBM)


def transform_kernel(counts_ref, table_ref, columns_ref, out_ref, buf, table, limits, *sems):
    members, each, bands, length = out_ref.shape
    steps = buf.shape[0]
    span = buf.shape[2]
    per_member = each // GROUP
    read_sems, table_sem, counts_sem = sems

    def fetch(i):
        rows = pl.ds(pl.multiple_of(i * span, span), span)
        return pltpu.make_async_copy(columns_ref.at[:, rows, :], buf.at[i], read_sems.at[i])

    counts_copy = pltpu.make_async_copy(counts_ref, limits, counts_sem)
    table_copy = pltpu.make_async_copy(table_ref, table, table_sem)
    counts_copy.start()
    table_copy.start()
    for i in range(steps):
        fetch(i).start()
    counts_copy.wait()
    limit = limits[lax.axis_index("pw")]
    live_steps = lax.div(limit + span - 1, span)
    reached = live_steps * (span // GROUP)

    def step(i, carry):
        fetch(i).wait()
        for part in range(span // GROUP):
            start = part * GROUP
            rows = buf[i, :, start : start + GROUP, :]
            turned = jnp.swapaxes(rows, 0, 1).reshape(GROUP * bands, length)
            value = dot(turned, table[...]).astype(jnp.bfloat16)
            member = i * (span // each) + part // per_member
            first = part % per_member * GROUP
            out_ref[member, first : first + GROUP] = value.reshape(GROUP, bands, length)
        return carry

    def skip(i, carry):
        fetch(i).wait()
        return carry

    def clear_group(g, carry):
        first = pl.multiple_of(lax.rem(g, per_member) * GROUP, GROUP)
        zeros = jnp.zeros((GROUP, bands, length), jnp.bfloat16)
        out_ref[lax.div(g, per_member), pl.ds(first, GROUP)] = zeros
        return carry

    def clear_slot(s, carry):
        out_ref[lax.div(s, each), lax.rem(s, each)] = jnp.zeros((bands, length), jnp.bfloat16)
        return carry

    lax.fori_loop(reached, members * per_member, clear_group, 0)
    table_copy.wait()
    lax.fori_loop(0, live_steps, step, 0)
    whole = lax.div(limit + GROUP - 1, GROUP)
    lax.fori_loop(limit, whole * GROUP, clear_slot, 0)
    lax.fori_loop(whole, reached, clear_group, 0)
    lax.fori_loop(live_steps, steps, skip, 0)


def transform(columns, counts, members):
    bands, slots, length = columns.shape
    each = slots // members
    span = 2 * each
    steps = slots // span
    return pl.pallas_call(
        transform_kernel,
        in_specs=[pl.BlockSpec(memory_space=pltpu.HBM)] * 3,
        out_specs=pl.BlockSpec(memory_space=pltpu.VMEM),
        out_shape=jax.ShapeDtypeStruct((members, each, bands, length), jnp.bfloat16),
        scratch_shapes=[
            pltpu.VMEM((steps, bands, span, length), jnp.bfloat16),
            pltpu.VMEM((length, length), jnp.bfloat16),
            pltpu.SMEM(counts.shape, jnp.int32),
            pltpu.SemaphoreType.DMA((steps,)),
            pltpu.SemaphoreType.DMA,
            pltpu.SemaphoreType.DMA,
        ],
        compiler_params=params(44),
        name="transform",
    )(in_hbm(counts), in_hbm(hartley(length)), in_hbm(columns))


def gram_kernel(each, sticks_ref, out_ref):
    members, slots, bands, length = sticks_ref.shape
    total = members * bands
    acc = jnp.zeros((total, total), jnp.float32)
    for i in range(0, slots, each):
        rows = [sticks_ref[:, i + s].reshape(total, length) for s in range(each)]
        wide = jnp.concatenate(rows, axis=1)
        acc += lax.dot_general(
            wide, wide, (((1,), (1,)), ((), ())), preferred_element_type=jnp.float32
        )
    piece = 0
    for r in range(0, total, 8):
        for c in range(0, total, 128):
            for half in range(2):
                out_ref[piece] = acc[r + 4 * half : r + 4 * half + 4, c : c + 128]
                piece += 1


def gram(sticks, each):
    members, slots, bands, length = sticks.shape
    total = members * bands
    return pl.pallas_call(
        functools.partial(gram_kernel, each),
        in_specs=[pl.BlockSpec(memory_space=pltpu.VMEM)],
        out_specs=pl.BlockSpec(memory_space=pltpu.VMEM),
        out_shape=jax.ShapeDtypeStruct((total * total // 512, 4, 128), jnp.float32),
        compiler_params=params(20),
        name="gram",
    )(sticks)


def spread_kernel(shares_ref, out_ref):
    share = jnp.sum(shares_ref[...], axis=0, keepdims=True)
    out_ref[...] = jnp.broadcast_to(share, out_ref.shape)


def spread(shares):
    return pl.pallas_call(
        spread_kernel,
        in_specs=[pl.BlockSpec(memory_space=pltpu.VMEM)],
        out_specs=pl.BlockSpec(memory_space=pltpu.VMEM),
        out_shape=jax.ShapeDtypeStruct(shares.shape, shares.dtype),
        compiler_params=params(8),
        name="spread",
    )(shares)


def split(value):
    high = value.astype(jnp.bfloat16)
    return high, (value - high.astype(jnp.float32)).astype(jnp.bfloat16)


def product(left, right):
    left_high, left_low = left
    right_high, right_low = right
    both = dot(jnp.concatenate([left_high, left_low], axis=0), right_high)
    rows = left_high.shape[0]
    return both[:rows] + (both[rows:] + dot(left_high, right_low))


def rotate_kernel(counts_ref, sums_ref, sticks_ref, out_ref, turn_ref):
    members, slots, bands, length = sticks_ref.shape
    size = members * bands
    live = counts_ref[0]
    for i in range(1, counts_ref.shape[0]):
        live += counts_ref[i]
    tiles = size // 128
    pieces = [sums_ref[i] for i in range(sums_ref.shape[0])]
    whole = [jnp.concatenate(pieces[i : i + 2], axis=0) for i in range(0, len(pieces), 2)]
    lines = [jnp.concatenate(whole[i : i + tiles], axis=1) for i in range(0, len(whole), tiles)]
    correlation = jnp.concatenate(lines, axis=0) / (live.astype(jnp.float32) * length)
    row = lax.broadcasted_iota(jnp.int32, (size, size), 0)
    col = lax.broadcasted_iota(jnp.int32, (size, size), 1)
    ident = jnp.where(row == col, 1.0, 0.0)
    scale = jnp.sum(correlation * ident, keepdims=True) / size
    y_iter = correlation / scale

    t_iter = y_iter
    z_iter = 1.5 * ident - 0.5 * t_iter
    p_split = split(z_iter)
    for step in range(1, ITERS):
        half = product(split(t_iter), p_split)
        t_iter = product(split(half), p_split)
        p_split = split(1.5 * ident - 0.5 * t_iter)
        z_iter = product(p_split, split(z_iter))
    turn_ref[...] = (z_iter / jnp.sqrt(scale)).T.astype(jnp.bfloat16)

    turn = turn_ref[...]
    for s in range(slots):
        value = dot(turn, sticks_ref[:, s].reshape(size, length)).astype(jnp.bfloat16)
        out_ref[:, s] = value.reshape(members, bands, length)


def rotate(counts, sums, sticks):
    members, slots, bands, length = sticks.shape
    size = members * bands
    return pl.pallas_call(
        rotate_kernel,
        in_specs=[
            pl.BlockSpec(memory_space=pltpu.SMEM),
            pl.BlockSpec(memory_space=pltpu.VMEM),
            pl.BlockSpec(memory_space=pltpu.VMEM),
        ],
        out_specs=pl.BlockSpec(memory_space=pltpu.VMEM),
        out_shape=jax.ShapeDtypeStruct(sticks.shape, jnp.bfloat16),
        scratch_shapes=[pltpu.VMEM((size, size), jnp.bfloat16)],
        compiler_params=params(24),
        name="rotate",
    )(counts, sums, sticks)


def place_kernel(in_ref, out_ref, buf, sems):
    members, each, bands, length = in_ref.shape

    def store(i):
        rows = pl.ds(pl.multiple_of(i * each, each), each)
        return pltpu.make_async_copy(buf.at[i], out_ref.at[:, rows, :], sems.at[i])

    def step(i, carry):
        for s in range(0, each, GROUP):
            buf[i, :, s : s + GROUP, :] = jnp.swapaxes(in_ref[i, s : s + GROUP], 0, 1)
        store(i).start()
        return carry

    def finish(i, carry):
        store(i).wait()
        return carry

    lax.fori_loop(0, members, step, 0)
    lax.fori_loop(0, members, finish, 0)


def place(rotated):
    members, each, bands, length = rotated.shape
    return pl.pallas_call(
        place_kernel,
        in_specs=[pl.BlockSpec(memory_space=pltpu.VMEM)],
        out_specs=pl.BlockSpec(memory_space=pltpu.HBM),
        out_shape=jax.ShapeDtypeStruct((bands, members * each, length), jnp.bfloat16),
        scratch_shapes=[
            pltpu.VMEM((members, bands, each, length), jnp.bfloat16),
            pltpu.SemaphoreType.DMA((members,)),
        ],
        compiler_params=params(32),
        name="place",
    )(rotated)


def make_local(members):
    def local(columns, counts):
        def exchange(value, axes):
            return lax.all_to_all(value, axes, 0, 0, tiled=True)

        sticks = exchange(transform(columns, counts, members), "band")
        shares = exchange(gram(sticks, 16), ("band", "pw"))
        sums = exchange(spread(shares), ("band", "pw"))
        return place(exchange(rotate(counts, sums, sticks), "band"))

    return local


def solution(mesh):
    return jax.shard_map(
        make_local(mesh.shape["band"]),
        mesh=mesh,
        in_specs=(P("band", "pw", None), P()),
        out_specs=P("band", "pw", None),
        check_vma=False,
    )
```

```python
import functools

import jax
import jax.numpy as jnp
import numpy as np
from jax import lax
from jax.experimental import pallas as pl
from jax.experimental.pallas import tpu as pltpu
from jax.sharding import PartitionSpec as P

ITERS = 8
GROUP = 16
MIB = 1024 * 1024


def hartley(stick_length):
    rows = np.arange(stick_length, dtype=np.int32)
    phase = (rows[:, None] * rows[None, :] % stick_length).astype(np.float32)
    angle = phase * np.float32(2.0 * np.pi / stick_length)
    table = (np.cos(angle) + np.sin(angle)) / np.sqrt(np.float32(stick_length))
    return jnp.asarray(table.astype(jnp.bfloat16))


def dot(left, right):
    return jnp.dot(left, right, preferred_element_type=jnp.float32)


def params(mib):
    return pltpu.CompilerParams(vmem_limit_bytes=mib * MIB)


def in_hbm(value):
    return pltpu.with_memory_space_constraint(value, pltpu.HBM)


def transform_kernel(counts_ref, table_ref, columns_ref, out_ref, buf, table, limits, *sems):
    members, each, bands, length = out_ref.shape
    steps = buf.shape[0]
    span = buf.shape[2]
    per_member = each // GROUP
    read_sems, table_sem, counts_sem = sems

    def fetch(i):
        rows = pl.ds(pl.multiple_of(i * span, span), span)
        return pltpu.make_async_copy(columns_ref.at[:, rows, :], buf.at[i], read_sems.at[i])

    counts_copy = pltpu.make_async_copy(counts_ref, limits, counts_sem)
    table_copy = pltpu.make_async_copy(table_ref, table, table_sem)
    counts_copy.start()
    table_copy.start()
    for i in range(steps):
        fetch(i).start()
    counts_copy.wait()
    limit = limits[lax.axis_index("pw")]
    live_steps = lax.div(limit + span - 1, span)
    reached = live_steps * (span // GROUP)

    def step(i, carry):
        fetch(i).wait()
        for part in range(span // GROUP):
            start = part * GROUP
            rows = buf[i, :, start : start + GROUP, :]
            turned = jnp.swapaxes(rows, 0, 1).reshape(GROUP * bands, length)
            value = dot(turned, table[...]).astype(jnp.bfloat16)
            member = i * (span // each) + part // per_member
            first = part % per_member * GROUP
            out_ref[member, first : first + GROUP] = value.reshape(GROUP, bands, length)
        return carry

    def skip(i, carry):
        fetch(i).wait()
        return carry

    def clear_group(g, carry):
        first = pl.multiple_of(lax.rem(g, per_member) * GROUP, GROUP)
        zeros = jnp.zeros((GROUP, bands, length), jnp.bfloat16)
        out_ref[lax.div(g, per_member), pl.ds(first, GROUP)] = zeros
        return carry

    def clear_slot(s, carry):
        out_ref[lax.div(s, each), lax.rem(s, each)] = jnp.zeros((bands, length), jnp.bfloat16)
        return carry

    lax.fori_loop(reached, members * per_member, clear_group, 0)
    table_copy.wait()
    lax.fori_loop(0, live_steps, step, 0)
    whole = lax.div(limit + GROUP - 1, GROUP)
    lax.fori_loop(limit, whole * GROUP, clear_slot, 0)
    lax.fori_loop(whole, reached, clear_group, 0)
    lax.fori_loop(live_steps, steps, skip, 0)


def transform(columns, counts, members):
    bands, slots, length = columns.shape
    each = slots // members
    span = 4 * each
    steps = slots // span
    return pl.pallas_call(
        transform_kernel,
        in_specs=[pl.BlockSpec(memory_space=pltpu.HBM)] * 3,
        out_specs=pl.BlockSpec(memory_space=pltpu.VMEM),
        out_shape=jax.ShapeDtypeStruct((members, each, bands, length), jnp.bfloat16),
        scratch_shapes=[
            pltpu.VMEM((steps, bands, span, length), jnp.bfloat16),
            pltpu.VMEM((length, length), jnp.bfloat16),
            pltpu.SMEM(counts.shape, jnp.int32),
            pltpu.SemaphoreType.DMA((steps,)),
            pltpu.SemaphoreType.DMA,
            pltpu.SemaphoreType.DMA,
        ],
        compiler_params=params(44),
        name="transform",
    )(in_hbm(counts), in_hbm(hartley(length)), in_hbm(columns))


def gram_kernel(each, sticks_ref, out_ref):
    members, slots, bands, length = sticks_ref.shape
    total = members * bands
    acc = jnp.zeros((total, total), jnp.float32)
    for i in range(0, slots, each):
        rows = [sticks_ref[:, i + s].reshape(total, length) for s in range(each)]
        wide = jnp.concatenate(rows, axis=1)
        acc += lax.dot_general(
            wide, wide, (((1,), (1,)), ((), ())), preferred_element_type=jnp.float32
        )
    piece = 0
    for r in range(0, total, 8):
        for c in range(0, total, 128):
            for half in range(2):
                out_ref[piece] = acc[r + 4 * half : r + 4 * half + 4, c : c + 128]
                piece += 1


def gram(sticks, each):
    members, slots, bands, length = sticks.shape
    total = members * bands
    return pl.pallas_call(
        functools.partial(gram_kernel, each),
        in_specs=[pl.BlockSpec(memory_space=pltpu.VMEM)],
        out_specs=pl.BlockSpec(memory_space=pltpu.VMEM),
        out_shape=jax.ShapeDtypeStruct((total * total // 512, 4, 128), jnp.float32),
        compiler_params=params(20),
        name="gram",
    )(sticks)


def spread_kernel(shares_ref, out_ref):
    share = jnp.sum(shares_ref[...], axis=0, keepdims=True)
    out_ref[...] = jnp.broadcast_to(share, out_ref.shape)


def spread(shares):
    return pl.pallas_call(
        spread_kernel,
        in_specs=[pl.BlockSpec(memory_space=pltpu.VMEM)],
        out_specs=pl.BlockSpec(memory_space=pltpu.VMEM),
        out_shape=jax.ShapeDtypeStruct(shares.shape, shares.dtype),
        compiler_params=params(8),
        name="spread",
    )(shares)


def split(value):
    high = value.astype(jnp.bfloat16)
    return high, (value - high.astype(jnp.float32)).astype(jnp.bfloat16)


def product(left, right):
    left_high, left_low = left
    right_high, right_low = right
    both = dot(jnp.concatenate([left_high, left_low], axis=0), right_high)
    rows = left_high.shape[0]
    return both[:rows] + (both[rows:] + dot(left_high, right_low))


def rotate_kernel(counts_ref, sums_ref, sticks_ref, out_ref, turn_ref):
    members, slots, bands, length = sticks_ref.shape
    size = members * bands
    live = counts_ref[0]
    for i in range(1, counts_ref.shape[0]):
        live += counts_ref[i]
    tiles = size // 128
    pieces = [sums_ref[i] for i in range(sums_ref.shape[0])]
    whole = [jnp.concatenate(pieces[i : i + 2], axis=0) for i in range(0, len(pieces), 2)]
    lines = [jnp.concatenate(whole[i : i + tiles], axis=1) for i in range(0, len(whole), tiles)]
    correlation = jnp.concatenate(lines, axis=0) / (live.astype(jnp.float32) * length)
    row = lax.broadcasted_iota(jnp.int32, (size, size), 0)
    col = lax.broadcasted_iota(jnp.int32, (size, size), 1)
    ident = jnp.where(row == col, 1.0, 0.0)
    scale = jnp.sum(correlation * ident, keepdims=True) / size
    y_iter = correlation / scale

    t_iter = y_iter
    z_iter = 1.5 * ident - 0.5 * t_iter
    p_split = split(z_iter)
    for step in range(1, ITERS):
        half = product(split(t_iter), p_split)
        t_iter = product(split(half), p_split)
        p_split = split(1.5 * ident - 0.5 * t_iter)
        z_iter = product(p_split, split(z_iter))
    turn_ref[...] = (z_iter / jnp.sqrt(scale)).astype(jnp.bfloat16)

    turn = turn_ref[...]
    for s in range(slots):
        value = dot(turn, sticks_ref[:, s].reshape(size, length)).astype(jnp.bfloat16)
        out_ref[:, s] = value.reshape(members, bands, length)


def rotate(counts, sums, sticks):
    members, slots, bands, length = sticks.shape
    size = members * bands
    return pl.pallas_call(
        rotate_kernel,
        in_specs=[
            pl.BlockSpec(memory_space=pltpu.SMEM),
            pl.BlockSpec(memory_space=pltpu.VMEM),
            pl.BlockSpec(memory_space=pltpu.VMEM),
        ],
        out_specs=pl.BlockSpec(memory_space=pltpu.VMEM),
        out_shape=jax.ShapeDtypeStruct(sticks.shape, jnp.bfloat16),
        scratch_shapes=[pltpu.VMEM((size, size), jnp.bfloat16)],
        compiler_params=params(24),
        name="rotate",
    )(counts, sums, sticks)


def place_kernel(in_ref, out_ref, buf, sems):
    members, each, bands, length = in_ref.shape

    def store(i):
        rows = pl.ds(pl.multiple_of(i * each, each), each)
        return pltpu.make_async_copy(buf.at[i], out_ref.at[:, rows, :], sems.at[i])

    def step(i, carry):
        for s in range(0, each, GROUP):
            buf[i, :, s : s + GROUP, :] = jnp.swapaxes(in_ref[i, s : s + GROUP], 0, 1)
        store(i).start()
        return carry

    def finish(i, carry):
        store(i).wait()
        return carry

    lax.fori_loop(0, members, step, 0)
    lax.fori_loop(0, members, finish, 0)


def place(rotated):
    members, each, bands, length = rotated.shape
    return pl.pallas_call(
        place_kernel,
        in_specs=[pl.BlockSpec(memory_space=pltpu.VMEM)],
        out_specs=pl.BlockSpec(memory_space=pltpu.HBM),
        out_shape=jax.ShapeDtypeStruct((bands, members * each, length), jnp.bfloat16),
        scratch_shapes=[
            pltpu.VMEM((members, bands, each, length), jnp.bfloat16),
            pltpu.SemaphoreType.DMA((members,)),
        ],
        compiler_params=params(32),
        name="place",
    )(rotated)


def make_local(members):
    def local(columns, counts):
        def exchange(value, axes):
            return lax.all_to_all(value, axes, 0, 0, tiled=True)

        sticks = exchange(transform(columns, counts, members), "band")
        shares = exchange(gram(sticks, 32), ("band", "pw"))
        sums = exchange(spread(shares), ("band", "pw"))
        return place(exchange(rotate(counts, sums, sticks), "band"))

    return local


def solution(mesh):
    return jax.shard_map(
        make_local(mesh.shape["band"]),
        mesh=mesh,
        in_specs=(P("band", "pw", None), P()),
        out_specs=P("band", "pw", None),
        check_vma=False,
    )
```

```python
import functools

import jax
import jax.numpy as jnp
import numpy as np
from jax import lax
from jax.experimental import pallas as pl
from jax.experimental.pallas import tpu as pltpu
from jax.sharding import PartitionSpec as P

ITERS = 8
GROUP = 16
MIB = 1024 * 1024


def hartley(stick_length):
    rows = np.arange(stick_length, dtype=np.int32)
    phase = (rows[:, None] * rows[None, :] % stick_length).astype(np.float32)
    angle = phase * np.float32(2.0 * np.pi / stick_length)
    table = (np.cos(angle) + np.sin(angle)) / np.sqrt(np.float32(stick_length))
    return jnp.asarray(table.astype(jnp.bfloat16))


def dot(left, right):
    return jnp.dot(left, right, preferred_element_type=jnp.float32)


def params(mib):
    return pltpu.CompilerParams(vmem_limit_bytes=mib * MIB)


def in_hbm(value):
    return pltpu.with_memory_space_constraint(value, pltpu.HBM)


def slot_chunks(slots):
    marks = [0, slots // 16, 3 * slots // 16, 7 * slots // 16, 11 * slots // 16, slots]
    marks = sorted({mark - mark % GROUP for mark in marks})
    return list(zip(marks[:-1], marks[1:]))


def transform_kernel(counts_ref, table_ref, columns_ref, out_ref, buf, table, limits, *sems):
    members, each, bands, length = out_ref.shape
    slots = buf.shape[1]
    per_member = each // GROUP
    read_sems, table_sem, counts_sem = sems
    chunks = slot_chunks(slots)

    def fetch(i):
        first, last = chunks[i]
        rows = pl.ds(first, last - first)
        return pltpu.make_async_copy(columns_ref.at[:, rows, :], buf.at[:, rows, :], read_sems.at[i])

    counts_copy = pltpu.make_async_copy(counts_ref, limits, counts_sem)
    table_copy = pltpu.make_async_copy(table_ref, table, table_sem)
    counts_copy.start()
    table_copy.start()
    for i in range(len(chunks)):
        fetch(i).start()
    counts_copy.wait()
    limit = limits[lax.axis_index("pw")]
    reached = 0
    for first, last in chunks:
        reached = jnp.where(limit > first, last // GROUP, reached)

    def clear_group(g, carry):
        first = pl.multiple_of(lax.rem(g, per_member) * GROUP, GROUP)
        zeros = jnp.zeros((GROUP, bands, length), jnp.bfloat16)
        out_ref[lax.div(g, per_member), pl.ds(first, GROUP)] = zeros
        return carry

    def clear_slot(s, carry):
        out_ref[lax.div(s, each), lax.rem(s, each)] = jnp.zeros((bands, length), jnp.bfloat16)
        return carry

    lax.fori_loop(reached, members * per_member, clear_group, 0)
    table_copy.wait()
    for i, (begin, end) in enumerate(chunks):
        fetch(i).wait()

        @pl.when(limit > begin)
        def _():
            for start in range(begin, end, GROUP):
                rows = buf[:, start : start + GROUP, :]
                turned = jnp.swapaxes(rows, 0, 1).reshape(GROUP * bands, length)
                value = dot(turned, table[...]).astype(jnp.bfloat16)
                first = start % each
                out_ref[start // each, first : first + GROUP] = value.reshape(GROUP, bands, length)

    whole = lax.div(limit + GROUP - 1, GROUP)
    lax.fori_loop(limit, whole * GROUP, clear_slot, 0)
    lax.fori_loop(whole, reached, clear_group, 0)


def transform(columns, counts, members):
    bands, slots, length = columns.shape
    each = slots // members
    steps = len(slot_chunks(slots))
    return pl.pallas_call(
        transform_kernel,
        in_specs=[pl.BlockSpec(memory_space=pltpu.HBM)] * 3,
        out_specs=pl.BlockSpec(memory_space=pltpu.VMEM),
        out_shape=jax.ShapeDtypeStruct((members, each, bands, length), jnp.bfloat16),
        scratch_shapes=[
            pltpu.VMEM((bands, slots, length), jnp.bfloat16),
            pltpu.VMEM((length, length), jnp.bfloat16),
            pltpu.SMEM(counts.shape, jnp.int32),
            pltpu.SemaphoreType.DMA((steps,)),
            pltpu.SemaphoreType.DMA,
            pltpu.SemaphoreType.DMA,
        ],
        compiler_params=params(44),
        name="transform",
    )(in_hbm(counts), in_hbm(hartley(length)), in_hbm(columns))


def gram_kernel(each, sticks_ref, out_ref):
    members, slots, bands, length = sticks_ref.shape
    total = members * bands
    acc = jnp.zeros((total, total), jnp.float32)
    for i in range(0, slots, each):
        rows = [sticks_ref[:, i + s].reshape(total, length) for s in range(each)]
        wide = jnp.concatenate(rows, axis=1)
        acc += lax.dot_general(
            wide, wide, (((1,), (1,)), ((), ())), preferred_element_type=jnp.float32
        )
    piece = 0
    for r in range(0, total, 8):
        for c in range(0, total, 128):
            for half in range(2):
                out_ref[piece] = acc[r + 4 * half : r + 4 * half + 4, c : c + 128]
                piece += 1


def gram(sticks, each):
    members, slots, bands, length = sticks.shape
    total = members * bands
    return pl.pallas_call(
        functools.partial(gram_kernel, each),
        in_specs=[pl.BlockSpec(memory_space=pltpu.VMEM)],
        out_specs=pl.BlockSpec(memory_space=pltpu.VMEM),
        out_shape=jax.ShapeDtypeStruct((total * total // 512, 4, 128), jnp.float32),
        compiler_params=params(20),
        name="gram",
    )(sticks)


def spread_kernel(shares_ref, out_ref):
    share = jnp.sum(shares_ref[...], axis=0, keepdims=True)
    out_ref[...] = jnp.broadcast_to(share, out_ref.shape)


def spread(shares):
    return pl.pallas_call(
        spread_kernel,
        in_specs=[pl.BlockSpec(memory_space=pltpu.VMEM)],
        out_specs=pl.BlockSpec(memory_space=pltpu.VMEM),
        out_shape=jax.ShapeDtypeStruct(shares.shape, shares.dtype),
        compiler_params=params(8),
        name="spread",
    )(shares)


def split(value):
    high = value.astype(jnp.bfloat16)
    return high, (value - high.astype(jnp.float32)).astype(jnp.bfloat16)


def product(left, right):
    left_high, left_low = left
    right_high, right_low = right
    both = dot(jnp.concatenate([left_high, left_low], axis=0), right_high)
    rows = left_high.shape[0]
    return both[:rows] + (both[rows:] + dot(left_high, right_low))


def rotate_kernel(counts_ref, sums_ref, sticks_ref, out_ref, turn_ref):
    members, slots, bands, length = sticks_ref.shape
    size = members * bands
    live = counts_ref[0]
    for i in range(1, counts_ref.shape[0]):
        live += counts_ref[i]
    tiles = size // 128
    pieces = [sums_ref[i] for i in range(sums_ref.shape[0])]
    whole = [jnp.concatenate(pieces[i : i + 2], axis=0) for i in range(0, len(pieces), 2)]
    lines = [jnp.concatenate(whole[i : i + tiles], axis=1) for i in range(0, len(whole), tiles)]
    correlation = jnp.concatenate(lines, axis=0) / (live.astype(jnp.float32) * length)
    row = lax.broadcasted_iota(jnp.int32, (size, size), 0)
    col = lax.broadcasted_iota(jnp.int32, (size, size), 1)
    ident = jnp.where(row == col, 1.0, 0.0)
    scale = jnp.sum(correlation * ident, keepdims=True) / size
    y_iter = correlation / scale

    t_iter = y_iter
    z_iter = 1.5 * ident - 0.5 * t_iter
    p_split = split(z_iter)
    for step in range(1, ITERS):
        half = product(split(t_iter), p_split)
        t_iter = product(split(half), p_split)
        p_split = split(1.5 * ident - 0.5 * t_iter)
        z_iter = product(p_split, split(z_iter))
    turn_ref[...] = (z_iter / jnp.sqrt(scale)).astype(jnp.bfloat16)

    turn = turn_ref[...]
    for s in range(slots):
        value = dot(turn, sticks_ref[:, s].reshape(size, length)).astype(jnp.bfloat16)
        out_ref[:, s] = value.reshape(members, bands, length)


def rotate(counts, sums, sticks):
    members, slots, bands, length = sticks.shape
    size = members * bands
    return pl.pallas_call(
        rotate_kernel,
        in_specs=[
            pl.BlockSpec(memory_space=pltpu.SMEM),
            pl.BlockSpec(memory_space=pltpu.VMEM),
            pl.BlockSpec(memory_space=pltpu.VMEM),
        ],
        out_specs=pl.BlockSpec(memory_space=pltpu.VMEM),
        out_shape=jax.ShapeDtypeStruct(sticks.shape, jnp.bfloat16),
        scratch_shapes=[pltpu.VMEM((size, size), jnp.bfloat16)],
        compiler_params=params(24),
        name="rotate",
    )(counts, sums, sticks)


def place_kernel(in_ref, out_ref, buf, sems):
    members, each, bands, length = in_ref.shape

    def store(i):
        rows = pl.ds(pl.multiple_of(i * each, each), each)
        return pltpu.make_async_copy(buf.at[i], out_ref.at[:, rows, :], sems.at[i])

    def step(i, carry):
        for s in range(0, each, GROUP):
            buf[i, :, s : s + GROUP, :] = jnp.swapaxes(in_ref[i, s : s + GROUP], 0, 1)
        store(i).start()
        return carry

    def finish(i, carry):
        store(i).wait()
        return carry

    lax.fori_loop(0, members, step, 0)
    lax.fori_loop(0, members, finish, 0)


def place(rotated):
    members, each, bands, length = rotated.shape
    return pl.pallas_call(
        place_kernel,
        in_specs=[pl.BlockSpec(memory_space=pltpu.VMEM)],
        out_specs=pl.BlockSpec(memory_space=pltpu.HBM),
        out_shape=jax.ShapeDtypeStruct((bands, members * each, length), jnp.bfloat16),
        scratch_shapes=[
            pltpu.VMEM((members, bands, each, length), jnp.bfloat16),
            pltpu.SemaphoreType.DMA((members,)),
        ],
        compiler_params=params(32),
        name="place",
    )(rotated)


def make_local(members):
    def local(columns, counts):
        def exchange(value, axes):
            return lax.all_to_all(value, axes, 0, 0, tiled=True)

        sticks = exchange(transform(columns, counts, members), "band")
        shares = exchange(gram(sticks, 32), ("band", "pw"))
        sums = exchange(spread(shares), ("band", "pw"))
        return place(exchange(rotate(counts, sums, sticks), "band"))

    return local


def solution(mesh):
    return jax.shard_map(
        make_local(mesh.shape["band"]),
        mesh=mesh,
        in_specs=(P("band", "pw", None), P()),
        out_specs=P("band", "pw", None),
        check_vma=False,
    )
```

```python
import functools

import jax
import jax.numpy as jnp
import numpy as np
from jax import lax
from jax.experimental import pallas as pl
from jax.experimental.pallas import tpu as pltpu
from jax.sharding import PartitionSpec as P

ITERS = 8
GROUP = 16
MIB = 1024 * 1024


def hartley(stick_length):
    rows = np.arange(stick_length, dtype=np.int32)
    phase = (rows[:, None] * rows[None, :] % stick_length).astype(np.float32)
    angle = phase * np.float32(2.0 * np.pi / stick_length)
    table = (np.cos(angle) + np.sin(angle)) / np.sqrt(np.float32(stick_length))
    return jnp.asarray(table.astype(jnp.bfloat16))


def dot(left, right):
    return jnp.dot(left, right, preferred_element_type=jnp.float32)


def params(mib):
    return pltpu.CompilerParams(vmem_limit_bytes=mib * MIB)


def in_hbm(value):
    return pltpu.with_memory_space_constraint(value, pltpu.HBM)


def slot_chunks(slots):
    marks = [part * slots // 16 for part in (0, 1, 3, 6, 9, 12, 16)]
    marks = sorted({mark - mark % GROUP for mark in marks})
    return list(zip(marks[:-1], marks[1:]))


def transform_kernel(counts_ref, table_ref, columns_ref, out_ref, buf, table, limits, *sems):
    members, each, bands, length = out_ref.shape
    slots = buf.shape[1]
    per_member = each // GROUP
    read_sems, table_sem, counts_sem = sems
    chunks = slot_chunks(slots)

    def fetch(i):
        first, last = chunks[i]
        rows = pl.ds(first, last - first)
        return pltpu.make_async_copy(columns_ref.at[:, rows, :], buf.at[:, rows, :], read_sems.at[i])

    counts_copy = pltpu.make_async_copy(counts_ref, limits, counts_sem)
    table_copy = pltpu.make_async_copy(table_ref, table, table_sem)
    counts_copy.start()
    table_copy.start()
    for i in range(len(chunks)):
        fetch(i).start()
    def clear_group(g, carry):
        first = pl.multiple_of(lax.rem(g, per_member) * GROUP, GROUP)
        zeros = jnp.zeros((GROUP, bands, length), jnp.bfloat16)
        out_ref[lax.div(g, per_member), pl.ds(first, GROUP)] = zeros
        return carry

    def clear_slot(s, carry):
        out_ref[lax.div(s, each), lax.rem(s, each)] = jnp.zeros((bands, length), jnp.bfloat16)
        return carry

    def work(begin, end):
        for start in range(begin, end, GROUP):
            rows = buf[:, start : start + GROUP, :]
            turned = jnp.swapaxes(rows, 0, 1).reshape(GROUP * bands, length)
            value = dot(turned, table[...]).astype(jnp.bfloat16)
            first = start % each
            out_ref[start // each, first : first + GROUP] = value.reshape(GROUP, bands, length)

    table_copy.wait()
    fetch(0).wait()
    work(*chunks[0])
    counts_copy.wait()
    limit = limits[lax.axis_index("pw")]
    reached = 0
    for first, last in chunks:
        reached = jnp.where(limit > first, last // GROUP, reached)
    lax.fori_loop(reached, members * per_member, clear_group, 0)
    for i in range(1, len(chunks)):
        fetch(i).wait()
        pl.when(limit > chunks[i][0])(functools.partial(work, *chunks[i]))

    whole = lax.div(limit + GROUP - 1, GROUP)
    lax.fori_loop(limit, whole * GROUP, clear_slot, 0)
    lax.fori_loop(whole, reached, clear_group, 0)


def transform(columns, counts, members):
    bands, slots, length = columns.shape
    each = slots // members
    steps = len(slot_chunks(slots))
    return pl.pallas_call(
        transform_kernel,
        in_specs=[pl.BlockSpec(memory_space=pltpu.HBM)] * 3,
        out_specs=pl.BlockSpec(memory_space=pltpu.VMEM),
        out_shape=jax.ShapeDtypeStruct((members, each, bands, length), jnp.bfloat16),
        scratch_shapes=[
            pltpu.VMEM((bands, slots, length), jnp.bfloat16),
            pltpu.VMEM((length, length), jnp.bfloat16),
            pltpu.SMEM(counts.shape, jnp.int32),
            pltpu.SemaphoreType.DMA((steps,)),
            pltpu.SemaphoreType.DMA,
            pltpu.SemaphoreType.DMA,
        ],
        compiler_params=params(44),
        name="transform",
    )(in_hbm(counts), in_hbm(hartley(length)), in_hbm(columns))


def gram_kernel(each, sticks_ref, out_ref):
    members, slots, bands, length = sticks_ref.shape
    total = members * bands
    acc = jnp.zeros((total, total), jnp.float32)
    for i in range(0, slots, each):
        rows = [sticks_ref[:, i + s].reshape(total, length) for s in range(each)]
        wide = jnp.concatenate(rows, axis=1)
        acc += lax.dot_general(
            wide, wide, (((1,), (1,)), ((), ())), preferred_element_type=jnp.float32
        )
    piece = 0
    for r in range(0, total, 8):
        for c in range(0, total, 128):
            for half in range(2):
                out_ref[piece] = acc[r + 4 * half : r + 4 * half + 4, c : c + 128]
                piece += 1


def gram(sticks, each):
    members, slots, bands, length = sticks.shape
    total = members * bands
    return pl.pallas_call(
        functools.partial(gram_kernel, each),
        in_specs=[pl.BlockSpec(memory_space=pltpu.VMEM)],
        out_specs=pl.BlockSpec(memory_space=pltpu.VMEM),
        out_shape=jax.ShapeDtypeStruct((total * total // 512, 4, 128), jnp.float32),
        compiler_params=params(20),
        name="gram",
    )(sticks)


def spread_kernel(shares_ref, out_ref):
    share = jnp.sum(shares_ref[...], axis=0, keepdims=True)
    out_ref[...] = jnp.broadcast_to(share, out_ref.shape)


def spread(shares):
    return pl.pallas_call(
        spread_kernel,
        in_specs=[pl.BlockSpec(memory_space=pltpu.VMEM)],
        out_specs=pl.BlockSpec(memory_space=pltpu.VMEM),
        out_shape=jax.ShapeDtypeStruct(shares.shape, shares.dtype),
        compiler_params=params(8),
        name="spread",
    )(shares)


def split(value):
    high = value.astype(jnp.bfloat16)
    return high, (value - high.astype(jnp.float32)).astype(jnp.bfloat16)


def product(left, right):
    left_high, left_low = left
    right_high, right_low = right
    both = dot(jnp.concatenate([left_high, left_low], axis=0), right_high)
    rows = left_high.shape[0]
    return both[:rows] + (both[rows:] + dot(left_high, right_low))


def rotate_kernel(counts_ref, sums_ref, sticks_ref, out_ref, turn_ref):
    members, slots, bands, length = sticks_ref.shape
    size = members * bands
    live = counts_ref[0]
    for i in range(1, counts_ref.shape[0]):
        live += counts_ref[i]
    tiles = size // 128
    pieces = [sums_ref[i] for i in range(sums_ref.shape[0])]
    whole = [jnp.concatenate(pieces[i : i + 2], axis=0) for i in range(0, len(pieces), 2)]
    lines = [jnp.concatenate(whole[i : i + tiles], axis=1) for i in range(0, len(whole), tiles)]
    correlation = jnp.concatenate(lines, axis=0) / (live.astype(jnp.float32) * length)
    row = lax.broadcasted_iota(jnp.int32, (size, size), 0)
    col = lax.broadcasted_iota(jnp.int32, (size, size), 1)
    ident = jnp.where(row == col, 1.0, 0.0)
    scale = jnp.sum(correlation * ident, keepdims=True) / size
    y_iter = correlation / scale

    t_iter = y_iter
    z_iter = 1.5 * ident - 0.5 * t_iter
    p_split = split(z_iter)
    for step in range(1, ITERS):
        half = product(split(t_iter), p_split)
        t_iter = product(split(half), p_split)
        p_split = split(1.5 * ident - 0.5 * t_iter)
        z_iter = product(p_split, split(z_iter))
    turn_ref[...] = (z_iter / jnp.sqrt(scale)).astype(jnp.bfloat16)

    turn = turn_ref[...]
    for s in range(slots):
        value = dot(turn, sticks_ref[:, s].reshape(size, length)).astype(jnp.bfloat16)
        out_ref[:, s] = value.reshape(members, bands, length)


def rotate(counts, sums, sticks):
    members, slots, bands, length = sticks.shape
    size = members * bands
    return pl.pallas_call(
        rotate_kernel,
        in_specs=[
            pl.BlockSpec(memory_space=pltpu.SMEM),
            pl.BlockSpec(memory_space=pltpu.VMEM),
            pl.BlockSpec(memory_space=pltpu.VMEM),
        ],
        out_specs=pl.BlockSpec(memory_space=pltpu.VMEM),
        out_shape=jax.ShapeDtypeStruct(sticks.shape, jnp.bfloat16),
        scratch_shapes=[pltpu.VMEM((size, size), jnp.bfloat16)],
        compiler_params=params(24),
        name="rotate",
    )(counts, sums, sticks)


def place_kernel(in_ref, out_ref, buf, sems):
    members, each, bands, length = in_ref.shape

    def store(i):
        rows = pl.ds(pl.multiple_of(i * each, each), each)
        return pltpu.make_async_copy(buf.at[i], out_ref.at[:, rows, :], sems.at[i])

    def step(i, carry):
        for s in range(0, each, GROUP):
            buf[i, :, s : s + GROUP, :] = jnp.swapaxes(in_ref[i, s : s + GROUP], 0, 1)
        store(i).start()
        return carry

    def finish(i, carry):
        store(i).wait()
        return carry

    lax.fori_loop(0, members, step, 0)
    lax.fori_loop(0, members, finish, 0)


def place(rotated):
    members, each, bands, length = rotated.shape
    return pl.pallas_call(
        place_kernel,
        in_specs=[pl.BlockSpec(memory_space=pltpu.VMEM)],
        out_specs=pl.BlockSpec(memory_space=pltpu.HBM),
        out_shape=jax.ShapeDtypeStruct((bands, members * each, length), jnp.bfloat16),
        scratch_shapes=[
            pltpu.VMEM((members, bands, each, length), jnp.bfloat16),
            pltpu.SemaphoreType.DMA((members,)),
        ],
        compiler_params=params(32),
        name="place",
    )(rotated)


def make_local(members):
    def local(columns, counts):
        def exchange(value, axes):
            return lax.all_to_all(value, axes, 0, 0, tiled=True)

        sticks = exchange(transform(columns, counts, members), "band")
        shares = exchange(gram(sticks, 32), ("band", "pw"))
        sums = exchange(spread(shares), ("band", "pw"))
        return place(exchange(rotate(counts, sums, sticks), "band"))

    return local


def solution(mesh):
    return jax.shard_map(
        make_local(mesh.shape["band"]),
        mesh=mesh,
        in_specs=(P("band", "pw", None), P()),
        out_specs=P("band", "pw", None),
        check_vma=False,
    )
```
